32 devices in a mesh: groups: 2 (over x), expert: 4 (over y, core), dp: 4 (over z).
Axes of the slice: x: 2, y: 2, z: 4, core: 2. Of those that a mesh axis runs over, the one named last changes fastest.
Arguments:
- tokens: bfloat16 [4096, 3584], P(('groups', 'expert', 'dp')), parts along dimension 0, may hold values from -6 to 6
- routes: int32 [4096, 1], P(('groups', 'expert', 'dp')), parts along dimension 0, may hold values from 0 to 3; in each aligned block of 128 rows (0 to 127, 128 to 255, ...) at most 48 rows name the same one
- gates: float32 [4096, 1], P(('groups', 'expert', 'dp')), parts along dimension 0, may hold values from 0.25 to 1
- gate_weight: bfloat16 [4, 3584, 1024], P('expert', 'dp'), may hold values from -0.09375 to 0.09375
- up_weight: bfloat16 [4, 3584, 1024], P('expert', 'dp'), may hold values from -0.09375 to 0.09375
- down_weight: bfloat16 [4, 3584, 1024], P('expert', 'dp'), may hold values from -0.1875 to 0.1875
- cotangent: bfloat16 [4096, 3584], P(('groups', 'expert', 'dp')), parts along dimension 0, may hold values from -6 to 6
Outputs:
- mixed: bfloat16 [4096, 3584], P(('groups', 'expert', 'dp')), parts along dimension 0
- token_grad: bfloat16 [4096, 3584], P(('groups', 'expert', 'dp')), parts along dimension 0
- gate_grad: bfloat16 [8, 3584, 1024], P(('groups', 'expert'), 'dp'), parts along dimension 0
- up_grad: bfloat16 [8, 3584, 1024], P(('groups', 'expert'), 'dp'), parts along dimension 0
- down_grad: bfloat16 [8, 3584, 1024], P(('groups', 'expert'), 'dp'), parts along dimension 0
The draws below stay inside these ranges and needn't reach their ends.
There are 2 independent parts, one for each index of `groups`. The reference program is written for one: setup_inputs(seed, part) draws one part's arguments, and reference() takes and returns one part's arrays. A program takes and returns all parts, laid end to end along the dimension named above; an argument that names none is the same for every part. Nothing has to cross between parts.
Inputs may be any that keep to these rules, and one draw needn't show every extreme that they name: Each token is routed to exactly one expert. The routes of one device's 128 tokens name one expert at most 48 times, and in every draw some expert is named exactly 48 times by some device.
All inputs are finite; a program needn't handle non-finite values.
Results may differ from the reference program's by a relative error of at most 0.0058.
Values may be sent and summed in bfloat16 or wider, within the bound.
No kernel may reach another device: no remote copies, remote signals or barrier semaphores. Data moves between devices by JAX's collectives and lax.ppermute only.
A program may use at most 256 MiB of HBM per device.

```python
import math
import jax
import jax.numpy as jnp
import numpy as np
from jax import lax

D = 3584
FF = 1024
TOK_DEV = 128
TOPK = 1
EXPERTS = 4
CAP = 48
TOKENS = 2048
N_EXPERT = 4
N_DP = 4


def levels(key, shape, shards, smallest, high):
    def one(axis_at, blocks):
        heights = jax.random.uniform(jax.random.fold_in(jax.random.fold_in(key, 6), axis_at), (blocks,), jnp.float32, smallest / len(shards), high / len(shards))
        return jnp.repeat(jnp.exp(heights), shape[axis_at] // blocks).reshape((-1,) + (1,) * (len(shape) - axis_at - 1))

    gain = one(*shards[0])
    for cut in shards[1:]:
        gain = gain * one(*cut)
    return gain


def assign_block(stream_key, own, number, rows, number_of, top, bound, slope):
    order = jax.random.permutation(stream_key, number_of)
    packed, usual = portions_of(number_of, rows * top, bound, slope, True), portions_of(number_of, rows * top, bound, slope, False)
    places = jnp.arange(number_of)

    def named(tallies, turn):
        used = int((tallies > 0).sum())
        fixed = max(1, used // 4)
        passed = fixed + (places - fixed + turn * (used - fixed)) % max(1, number_of - fixed)
        return jnp.zeros((number_of,), jnp.int32).at[order[jnp.where(places < fixed, places, passed)]].set(jnp.asarray(tallies, jnp.int32))

    tallies = jnp.where(number % 4 == 0, named(packed, number // 4), named(usual, number - number // 4 - 1))
    mixed = jax.random.permutation(jax.random.fold_in(own, 3), number_of)
    donor, receiver = mixed[0:number_of // 2 * 2:2], mixed[1:number_of // 2 * 2:2]
    slack = jnp.minimum(tallies[donor] - 1, bound - tallies[receiver]) // 2
    slack = jnp.where((donor == order[0]) | (receiver == order[0]) | (tallies[receiver] == 0), 0, jnp.maximum(slack, 0))
    passed = jax.random.randint(jax.random.fold_in(own, 4), (number_of // 2,), 0, 1 << 20) % (slack + 1)
    tallies = tallies.at[donor].add(-passed).at[receiver].add(passed)
    items = jnp.searchsorted(jnp.cumsum(tallies), jnp.arange(rows * top), side="right").astype(jnp.int32)
    grid = items.reshape(top, rows).T
    grid = grid[jax.random.permutation(jax.random.fold_in(own, 1), rows)]
    turn = jax.random.randint(jax.random.fold_in(own, 2), (rows, 1), 0, top)
    return jnp.take_along_axis(grid, (jnp.arange(top)[None, :] + turn) % top, axis=1)


def portions_of(amount, total, bound, slope, full):
    portions = [(1 << 20) // math.isqrt(standing ** slope) + 1 for standing in range(1, amount + 1)]
    largest = bound if full else min(bound, max(-(-total // amount), total * portions[0] // sum(portions)))
    least = 1 if total - largest >= amount - 1 else 0
    counts, rest = [largest] + [least] * (amount - 1), total - largest - least * (amount - 1)
    while rest > 0:
        candidates = [i for i in range(1, amount) if counts[i] < largest] or [i for i in range(1, amount) if counts[i] < bound]
        pool, left = sum([portions[i] for i in candidates]), rest
        for i in candidates:
            addition = min(bound - counts[i], max(1, left * portions[i] // pool), rest)
            counts[i] = counts[i] + addition
            rest = rest - addition
    return np.array(counts)


def normal_values(key, extent, width, bound, pieces=(), kind=jnp.bfloat16):
    entries = jax.random.normal(key, extent, jnp.float32) * width
    if len(pieces) > 0:
        entries = levels(key, extent, pieces, -0.22, 0.18) * entries
    return jnp.clip(entries, min=-bound, max=bound).astype(kind)


def setup_inputs(seed: int = 0, part: int = 0) -> dict:
    key_list = jax.random.split(jax.random.key(seed), 8)
    own_keys = jax.random.split(jax.random.fold_in(key_list[7], part), 8)
    tokens = normal_values(own_keys[0], (TOKENS, D), 1.0, 6.0, ((0, 16),))
    routes_keys = jax.random.split(jax.random.fold_in(own_keys[1], 1), TOKENS // TOK_DEV)
    routes_turns = jax.random.permutation(jax.random.fold_in(own_keys[1], 3), TOKENS // TOK_DEV)
    routes = jax.vmap(lambda own, number: assign_block(jax.random.fold_in(own_keys[1], 2), own, number, TOK_DEV, EXPERTS, TOPK, CAP, 2))(routes_keys, routes_turns).reshape((TOKENS, TOPK))
    gates = jnp.clip(0.25 + 0.75 * jax.random.uniform(own_keys[2], (TOKENS, TOPK), jnp.float32) ** levels(own_keys[2], (TOKENS, TOPK), ((0, 16),), -0.2, 0.2), 0.25, 1.0)
    gate_weight = normal_values(key_list[3], (EXPERTS, D, FF), D ** -0.5, 0.09375, ((0, 4), (1, 4)))
    up_weight = normal_values(key_list[4], (EXPERTS, D, FF), D ** -0.5, 0.09375, ((0, 4), (1, 4)))
    down_weight = normal_values(key_list[5], (EXPERTS, D, FF), FF ** -0.5, 0.1875, ((0, 4), (1, 4)))
    cotangent = normal_values(own_keys[6], (TOKENS, D), 1.0, 6.0, ((0, 16),))
    return dict(tokens=tokens, routes=routes, gates=gates, gate_weight=gate_weight, up_weight=up_weight, down_weight=down_weight, cotangent=cotangent)


def reference(tokens, routes, gates, gate_weight, up_weight, down_weight, cotangent):
    devices = N_EXPERT * N_DP
    flat_len = TOK_DEV * TOPK
    ids = routes.reshape(devices, flat_len)
    onehot = (ids[:, :, None] == jnp.arange(EXPERTS, dtype=jnp.int32)[None, None, :]).astype(jnp.int32)
    before = jnp.cumsum(onehot, axis=1) - onehot
    slot_pos = jnp.sum(before * onehot, axis=2).astype(jnp.int32)
    dest = (ids * CAP + slot_pos).astype(jnp.int32)
    block_ids = jnp.arange(devices, dtype=jnp.int32)
    entry = jnp.arange(flat_len, dtype=jnp.int32)[None, :] + (block_ids * flat_len)[:, None]
    table = jnp.full((devices, EXPERTS * CAP), TOKENS * TOPK, jnp.int32)
    table = table.at[block_ids[:, None], dest].set(entry)
    table = table.reshape(devices, EXPERTS, CAP).transpose(1, 0, 2).reshape(EXPERTS, devices * CAP)
    tokens_pad = jnp.concatenate([tokens, jnp.zeros((1, D), tokens.dtype)], axis=0)
    cot_pad = jnp.concatenate([cotangent, jnp.zeros((1, D), cotangent.dtype)], axis=0)
    gates_pad = jnp.concatenate([gates.reshape(-1), jnp.zeros((1,), gates.dtype)], axis=0)

    def one_expert(carry, inputs):
        out_acc, grad_acc = carry
        index, w_gate, w_up, w_down = inputs
        owner = index // TOPK
        rows = tokens_pad[owner]
        weight_of = gates_pad[index].astype(jnp.float32)
        pre_gate = jnp.dot(rows, w_gate, preferred_element_type=jnp.float32)
        pre_up = jnp.dot(rows, w_up, preferred_element_type=jnp.float32)
        sig = jax.nn.sigmoid(pre_gate)
        active = pre_gate * sig
        hidden = (active * pre_up).astype(jnp.bfloat16)
        expert_out = lax.dot_general(hidden, w_down, (((1,), (1,)), ((), ())), preferred_element_type=jnp.float32).astype(jnp.bfloat16)
        out_acc = out_acc.at[owner].add(weight_of[:, None] * expert_out.astype(jnp.float32))
        weighted = (weight_of[:, None] * cot_pad[owner].astype(jnp.float32)).astype(jnp.bfloat16)
        hidden_grad = jnp.dot(weighted, w_down, preferred_element_type=jnp.float32)
        pg_grad = (hidden_grad * pre_up * sig * (1.0 + pre_gate * (1.0 - sig))).astype(jnp.bfloat16)
        pu_grad = (hidden_grad * active).astype(jnp.bfloat16)
        row_grad = lax.dot_general(pg_grad, w_gate, (((1,), (1,)), ((), ())), preferred_element_type=jnp.float32)
        row_grad = row_grad + lax.dot_general(pu_grad, w_up, (((1,), (1,)), ((), ())), preferred_element_type=jnp.float32)
        row_grad = row_grad.astype(jnp.bfloat16)
        grad_acc = grad_acc.at[owner].add(row_grad.astype(jnp.float32))
        contract = (((0,), (0,)), ((), ()))
        g_gate = lax.dot_general(rows, pg_grad, contract, preferred_element_type=jnp.float32).astype(jnp.bfloat16)
        g_up = lax.dot_general(rows, pu_grad, contract, preferred_element_type=jnp.float32).astype(jnp.bfloat16)
        g_down = lax.dot_general(weighted, hidden, contract, preferred_element_type=jnp.float32).astype(jnp.bfloat16)
        return (out_acc, grad_acc), (g_gate, g_up, g_down)

    start = (jnp.zeros((TOKENS + 1, D), jnp.float32), jnp.zeros((TOKENS + 1, D), jnp.float32))
    (out_acc, grad_acc), (gate_grad, up_grad, down_grad) = lax.scan(one_expert, start, (table, gate_weight, up_weight, down_weight))
    mixed = out_acc[:TOKENS].astype(jnp.bfloat16)
    token_grad = grad_acc[:TOKENS].astype(jnp.bfloat16)
    return (mixed, token_grad, gate_grad, up_grad, down_grad)
```

```python
import jax
import jax.numpy as jnp
from jax import lax
from jax.sharding import PartitionSpec as P

F32 = jnp.float32
BF16 = jnp.bfloat16


def route_places(routes, experts, capacity):
    flat_ids = routes.reshape(-1)
    onehot = (flat_ids[:, None] == jnp.arange(experts, dtype=jnp.int32)[None, :]).astype(jnp.int32)
    before = jnp.cumsum(onehot, axis=0) - onehot
    slot_pos = jnp.sum(before * onehot, axis=1)
    return flat_ids * capacity + slot_pos


def across(left, right):
    return lax.dot_general(left, right, (((1,), (1,)), ((), ())), preferred_element_type=F32)


def over_rows(left, right):
    return lax.dot_general(left, right, (((0,), (0,)), ((), ())), preferred_element_type=F32)


def swap(value, axis, distance):
    count = lax.axis_size(axis)
    return lax.ppermute(value, axis, [(i, i ^ distance) for i in range(count)])


def line_sum(partial, axis):
    count = lax.axis_size(axis)
    total = partial
    for hop in range(count // 2 - 1):
        pairs = [(hop, hop + 1), (count - 1 - hop, count - 2 - hop)]
        total = partial + lax.ppermute(total.astype(BF16), axis, pairs).astype(F32)
    mid = count // 2
    return total + lax.ppermute(total.astype(BF16), axis, [(mid - 1, mid), (mid, mid - 1)]).astype(F32)


def line_spread(value, axis):
    count = lax.axis_size(axis)
    here = lax.axis_index(axis)
    for hop in reversed(range(count // 2 - 1)):
        pairs = [(hop + 1, hop), (count - 2 - hop, count - 1 - hop)]
        sent = lax.ppermute(value, axis, pairs)
        value = jnp.where((here == hop) | (here == count - 1 - hop), sent, value)
    return value


def shards(tokens, routes, gates, gate_weight, up_weight, down_weight, cotangent):
    n_exp = lax.axis_size("expert") * gate_weight.shape[0]
    n_dp = lax.axis_size("dp")
    me = lax.axis_index("expert")
    here = lax.axis_index("dp")
    tok_count, topk = routes.shape
    width = tokens.shape[1]
    part = width // n_dp
    hidden_units = gate_weight.shape[2]
    capacity = 3 * tok_count * topk // (2 * n_exp)
    chunk = n_dp * capacity
    w_gate, w_up, w_down = gate_weight[0], up_weight[0], down_weight[0]
    w_both = jnp.concatenate([w_gate, w_up], axis=1)

    codes = lax.all_gather(route_places(routes, n_exp, capacity), "dp")
    blocks = here ^ jnp.arange(n_dp, dtype=jnp.int32)
    codes = codes[blocks]
    places = ((codes // capacity) ^ me) * chunk + blocks[:, None] * capacity + codes % capacity
    places = places.reshape(-1)
    select = (jnp.arange(n_exp * chunk, dtype=jnp.int32)[:, None] == places[None, :]).astype(BF16)

    def columns(value, distance):
        return lax.dynamic_slice(value, (0, (here ^ distance) * part), (tok_count, part))

    def dispatch(pieces):
        gathered = jnp.concatenate(pieces, axis=0)
        rows = jnp.dot(select, gathered, preferred_element_type=F32).astype(BF16)
        rows = rows.reshape(n_exp, chunk, part)
        return [rows[0]] + [swap(rows[k], "expert", k) for k in range(1, n_exp)]

    weighted = (gates * cotangent.astype(F32)).astype(BF16)
    order = [0] + list(range(n_dp - 1, 0, -1))
    by_distance = {k: columns(tokens, k) if k == 0 else swap(columns(tokens, k), "dp", k) for k in order}
    rows = dispatch([by_distance[k] for k in range(n_dp)])
    by_distance = {k: columns(weighted, k) if k == 0 else swap(columns(weighted, k), "dp", k) for k in order}
    grads = dispatch([by_distance[k] for k in range(n_dp)])

    hidden, pg, pu, out, back = [], [], [], [], []
    for k in range(n_exp):
        pre = line_sum(jnp.dot(rows[k], w_both, preferred_element_type=F32), "dp")
        pre_gate, pre_up = pre[:, :hidden_units], pre[:, hidden_units:]
        sig = jax.nn.sigmoid(pre_gate)
        active = pre_gate * sig
        hidden.append(line_spread((active * pre_up).astype(BF16), "dp"))
        hidden_grad = line_sum(jnp.dot(grads[k], w_down, preferred_element_type=F32), "dp")
        pg_grad = (hidden_grad * pre_up * sig * (1.0 + pre_gate * (1.0 - sig))).astype(BF16)
        pu_grad = (hidden_grad * active).astype(BF16)
        both = line_spread(jnp.concatenate([pg_grad, pu_grad], axis=1), "dp")
        pg.append(both[:, :hidden_units])
        pu.append(both[:, hidden_units:])
        out_k = across(hidden[k], w_down).astype(BF16)
        back_k = across(both, w_both).astype(BF16)
        out.append(out_k if k == 0 else swap(out_k, "expert", k))
        back.append(back_k if k == 0 else swap(back_k, "expert", k))

    def give_back(parts_, scale):
        picked = over_rows(select, jnp.concatenate(parts_, axis=0)).astype(BF16).reshape(n_dp, tok_count, part)
        result = jnp.zeros((tok_count, width), BF16)
        for k in order:
            piece = picked[k] if k == 0 else swap(picked[k], "dp", k)
            if scale is not None:
                piece = (piece.astype(F32) * scale).astype(BF16)
            result = lax.dynamic_update_slice(result, piece, (0, (here ^ k) * part))
        return result

    mixed = give_back(out, gates)
    token_grad = give_back(back, None)
    all_rows, all_grads = jnp.concatenate(rows, axis=0), jnp.concatenate(grads, axis=0)
    gate_grad = over_rows(all_rows, jnp.concatenate(pg, axis=0)).astype(BF16)
    up_grad = over_rows(all_rows, jnp.concatenate(pu, axis=0)).astype(BF16)
    down_grad = over_rows(all_grads, jnp.concatenate(hidden, axis=0)).astype(BF16)
    return (mixed, token_grad, gate_grad[None], up_grad[None], down_grad[None])


def solution(mesh):
    rows = P(("groups", "expert", "dp"), None)
    weights = P("expert", "dp", None)
    grads = P(("groups", "expert"), "dp", None)
    return jax.shard_map(
        shards,
        mesh=mesh,
        in_specs=(rows, rows, rows, weights, weights, weights, rows),
        out_specs=(rows, rows, grads, grads, grads),
        check_vma=False,
    )
```

```python
import jax
import jax.numpy as jnp
from jax import lax
from jax.sharding import PartitionSpec as P

F32 = jnp.float32
BF16 = jnp.bfloat16
GROUPS = 4


def route_places(routes, experts, capacity):
    flat_ids = routes.reshape(-1)
    onehot = (flat_ids[:, None] == jnp.arange(experts, dtype=jnp.int32)[None, :]).astype(jnp.int32)
    before = jnp.cumsum(onehot, axis=0) - onehot
    slot_pos = jnp.sum(before * onehot, axis=1)
    return flat_ids * capacity + slot_pos


def across(left, right):
    return lax.dot_general(left, right, (((1,), (1,)), ((), ())), preferred_element_type=F32)


def over_rows(left, right):
    return lax.dot_general(left, right, (((0,), (0,)), ((), ())), preferred_element_type=F32)


def joined(values, axis=0):
    return values[0] if len(values) == 1 else jnp.concatenate(values, axis=axis)


class Queue:
    def __init__(self, axis, depth):
        self.axis, self.depth, self.arrived = axis, depth, []

    def send(self, value, pairs):
        if self.depth and len(self.arrived) >= self.depth:
            value, _ = lax.optimization_barrier((value, self.arrived[-self.depth]))
        got = lax.ppermute(value, self.axis, pairs)
        self.arrived.append(got)
        return got

    def swap(self, value, distance):
        count = lax.axis_size(self.axis)
        return self.send(value, [(i, i ^ distance) for i in range(count)])


class Line:
    def __init__(self, axis):
        self.count = lax.axis_size(axis)
        self.inward, self.middle, self.outward = Queue(axis, 1), Queue(axis, 2), Queue(axis, 1)

    def __call__(self, own):
        count, mid = self.count, self.count // 2
        total = own
        for hop in range(mid - 1):
            pairs = [(hop, hop + 1), (count - 1 - hop, count - 2 - hop)]
            total = total + self.inward.send(total.astype(BF16), pairs).astype(F32)
        got = self.middle.send(total.astype(BF16), [(mid - 1, mid), (mid, mid - 1)])
        for hop in reversed(range(mid - 1)):
            pairs = [(hop + 1, hop), (count - 2 - hop, count - 1 - hop)]
            got = got + self.outward.send((own + got.astype(F32)).astype(BF16), pairs)
        return total + got.astype(F32)


def shards(tokens, routes, gates, gate_weight, up_weight, down_weight, cotangent):
    n_exp = lax.axis_size("expert") * gate_weight.shape[0]
    n_dp = lax.axis_size("dp")
    me = lax.axis_index("expert")
    here = lax.axis_index("dp")
    tok_count, topk = routes.shape
    width = tokens.shape[1]
    part = width // n_dp
    hidden_units = gate_weight.shape[2]
    capacity = 3 * tok_count * topk // (2 * n_exp)
    chunk = n_dp * capacity
    per_group = n_exp // GROUPS
    w_gate, w_up, w_down = gate_weight[0], up_weight[0], down_weight[0]
    w_both = jnp.concatenate([w_gate, w_up], axis=1)
    distances = list(range(n_dp - 1, 0, -1))

    codes = lax.all_gather(route_places(routes, n_exp, capacity), "dp")
    blocks = here ^ jnp.arange(n_dp, dtype=jnp.int32)
    codes = codes[blocks]
    places = ((codes // capacity) ^ me) * chunk + blocks[:, None] * capacity + codes % capacity
    places = places.reshape(-1)
    select = (jnp.arange(n_exp * chunk, dtype=jnp.int32)[:, None] == places[None, :]).astype(BF16)

    features, experts = Queue("dp", n_dp - 1), Queue("expert", 0)

    def by_features(value):
        def columns(distance):
            return lax.dynamic_slice(value, (0, (here ^ distance) * part), (tok_count, part))

        got = {k: features.swap(columns(k), k) for k in distances}
        return jnp.concatenate([columns(0)] + [got[k] for k in range(1, n_dp)], axis=0)

    def dispatch(gathered):
        rows = jnp.dot(select, gathered, preferred_element_type=F32).astype(BF16)
        rows = rows.reshape(n_exp, chunk, part)
        rows = [rows[0]] + [experts.swap(rows[k], k) for k in range(1, n_exp)]
        return [joined(rows[g * per_group : (g + 1) * per_group]) for g in range(GROUPS)]

    rows = dispatch(by_features(tokens))
    grads = dispatch(by_features((gates * cotangent.astype(F32)).astype(BF16)))

    line = Line("dp")
    pre = [None] * GROUPS
    hid = [None] * GROUPS

    def first(g):
        pre[g] = line(jnp.dot(rows[g], w_both, preferred_element_type=F32))

    def second(g):
        hid[g] = line(jnp.dot(grads[g], w_down, preferred_element_type=F32))

    for step, g in ((first, 0), (second, 0), (first, 1), (second, 1), (first, 2), (first, 3), (second, 2), (second, 3)):
        step(g)

    hidden, both = [], []
    out, back = [], []
    for g in range(GROUPS):
        pre_gate, pre_up, hidden_grad = pre[g][:, :hidden_units], pre[g][:, hidden_units:], hid[g]
        sig = jax.nn.sigmoid(pre_gate)
        active = pre_gate * sig
        hidden.append((active * pre_up).astype(BF16))
        pg_grad = (hidden_grad * pre_up * sig * (1.0 + pre_gate * (1.0 - sig))).astype(BF16)
        pu_grad = (hidden_grad * active).astype(BF16)
        both.append(jnp.concatenate([pg_grad, pu_grad], axis=1))

    def returned(values, g):
        values = values.astype(BF16).reshape(per_group, chunk, part)
        values = [values[i] if k == 0 else experts.swap(values[i], k) for i, k in enumerate(range(g * per_group, (g + 1) * per_group))]
        return joined(values)

    for g in range(GROUPS):
        out.append(returned(across(hidden[g], w_down), g))
    for g in range(GROUPS):
        back.append(returned(across(both[g], w_both), g))

    def give_back(values, scale):
        picked = over_rows(select, jnp.concatenate(values, axis=0)).astype(BF16).reshape(n_dp, tok_count, part)
        result = jnp.zeros((tok_count, width), BF16)
        for k in [0] + distances:
            piece = picked[k] if k == 0 else features.swap(picked[k], k)
            if scale is not None:
                piece = (piece.astype(F32) * scale).astype(BF16)
            result = lax.dynamic_update_slice(result, piece, (0, (here ^ k) * part))
        return result

    mixed = give_back(out, gates)
    token_grad = give_back(back, None)
    all_rows, all_grads = jnp.concatenate(rows, axis=0), jnp.concatenate(grads, axis=0)
    all_both = over_rows(all_rows, jnp.concatenate(both, axis=0)).astype(BF16)
    down_grad = over_rows(all_grads, jnp.concatenate(hidden, axis=0)).astype(BF16)
    return (mixed, token_grad, all_both[:, :hidden_units][None], all_both[:, hidden_units:][None], down_grad[None])


def solution(mesh):
    rows = P(("groups", "expert", "dp"), None)
    weights = P("expert", "dp", None)
    grads = P(("groups", "expert"), "dp", None)
    return jax.shard_map(
        shards,
        mesh=mesh,
        in_specs=(rows, rows, rows, weights, weights, weights, rows),
        out_specs=(rows, rows, grads, grads, grads),
        check_vma=False,
    )
```

```python
import jax
import jax.numpy as jnp
from jax import lax
from jax.sharding import PartitionSpec as P

F32 = jnp.float32
BF16 = jnp.bfloat16
GROUPS = 4
CODE_ROWS = 16
AHEAD = 1
ITEMS = (("pre", (0,)), ("pre", (2,)), ("pre", (3,)), ("pre", (1,)), ("hid", (2, 3)), ("hid", (0, 1)))


def route_places(routes, experts, capacity):
    flat_ids = routes.reshape(-1)
    onehot = (flat_ids[:, None] == jnp.arange(experts, dtype=jnp.int32)[None, :]).astype(jnp.int32)
    before = jnp.cumsum(onehot, axis=0) - onehot
    slot_pos = jnp.sum(before * onehot, axis=1)
    return flat_ids * capacity + slot_pos


def across(left, right):
    return lax.dot_general(left, right, (((1,), (1,)), ((), ())), preferred_element_type=F32)


def over_rows(left, right):
    return lax.dot_general(left, right, (((0,), (0,)), ((), ())), preferred_element_type=F32)


def joined(values, axis=0):
    return values[0] if len(values) == 1 else jnp.concatenate(values, axis=axis)


def after(value, *others):
    return lax.optimization_barrier((value, *others))[0]


class Queue:
    def __init__(self, axis, depth):
        self.axis, self.depth, self.arrived = axis, depth, []

    def turn(self, value):
        return after(value, *self.arrived[-self.depth :][:1]) if len(self.arrived) >= self.depth > 0 else value

    def send(self, value, pairs):
        got = lax.ppermute(self.turn(value), self.axis, pairs)
        self.arrived.append(got)
        return got

    def swap(self, value, distance):
        count = lax.axis_size(self.axis)
        return self.send(value, [(i, i ^ distance) for i in range(count)])


class LineSum:
    def __init__(self, axis, own):
        self.axis, self.count, self.own, self.total = axis, lax.axis_size(axis), own, own
        self.got = None

    def inward(self):
        for hop in range(self.count // 2 - 1):
            pairs = [(hop, hop + 1), (self.count - 1 - hop, self.count - 2 - hop)]
            arrived = lax.ppermute(self.total.astype(BF16), self.axis, pairs)
            self.total = self.total + arrived.astype(F32)
        return arrived

    def middle(self):
        mid = self.count // 2
        self.got = lax.ppermute(self.total.astype(BF16), self.axis, [(mid - 1, mid), (mid, mid - 1)])
        return self.got

    def outward(self, *others):
        got = after(self.got, *others)
        for hop in reversed(range(self.count // 2 - 1)):
            pairs = [(hop + 1, hop), (self.count - 2 - hop, self.count - 1 - hop)]
            got = got + lax.ppermute((self.own + got.astype(F32)).astype(BF16), self.axis, pairs)
        self.got = got

    def result(self, *others):
        return self.total + after(self.got, *others).astype(F32)


def shards(tokens, routes, gates, gate_weight, up_weight, down_weight, cotangent):
    n_exp = lax.axis_size("expert") * gate_weight.shape[0]
    n_dp = lax.axis_size("dp")
    me = lax.axis_index("expert")
    here = lax.axis_index("dp")
    tok_count, topk = routes.shape
    width = tokens.shape[1]
    part = width // n_dp
    hidden_units = gate_weight.shape[2]
    capacity = 3 * tok_count * topk // (2 * n_exp)
    chunk = n_dp * capacity
    per_group = n_exp // GROUPS
    w_gate, w_up, w_down = gate_weight[0], up_weight[0], down_weight[0]
    w_both = jnp.concatenate([w_gate, w_up], axis=1)
    distances = list(range(n_dp - 1, 0, -1))

    features, experts = Queue("dp", 0), Queue("expert", 0)
    blocks = here ^ jnp.arange(n_dp, dtype=jnp.int32)

    def columns(value, distance):
        return lax.dynamic_slice(value, (0, (here ^ distance) * part), (tok_count, part))

    def by_features(value, tail):
        pieces = [columns(value, k) for k in range(n_dp)]
        if tail is not None:
            pieces = [jnp.concatenate([piece, tail], axis=0) for piece in pieces]
        earlier = list(features.arrived)
        got = {k: features.swap(after(pieces[k], *earlier), k) for k in distances}
        return [pieces[0]] + [got[k] for k in range(1, n_dp)]

    codes = route_places(routes, n_exp, capacity).astype(BF16)
    tail = jnp.zeros((CODE_ROWS, part), BF16) + jnp.pad(codes, (0, part - tok_count))[None, :]
    weighted = (gates * cotangent.astype(F32)).astype(BF16)
    got_rows = by_features(tokens, tail)
    got_grads = by_features(weighted, None)

    codes = jnp.stack([piece[tok_count, :tok_count] for piece in got_rows]).astype(jnp.int32)
    places = ((codes // capacity) ^ me) * chunk + blocks[:, None] * capacity + codes % capacity
    select = (jnp.arange(n_exp * chunk, dtype=jnp.int32)[:, None] == places.reshape(-1)[None, :]).astype(BF16)

    def dispatch(pieces):
        gathered = jnp.concatenate([piece[:tok_count] for piece in pieces], axis=0)
        rows = jnp.dot(select, gathered, preferred_element_type=F32).astype(BF16)
        return rows.reshape(n_exp, chunk, part)

    def exchange(blocks, bits, *others):
        blocks = list(blocks)
        for bit in bits:
            moved = [k for k in range(n_exp) if k & bit]
            sent = jnp.concatenate([blocks[k] for k in moved], axis=0)
            got = experts.swap(after(sent, *others), bit)
            for i, k in enumerate(moved):
                blocks[k] = got[i * chunk : (i + 1) * chunk]
            last = got
        return blocks, last

    bits = [n_exp >> (i + 1) for i in range(n_exp.bit_length() - 1)]

    def grouped(blocks):
        return [joined(blocks[g * per_group : (g + 1) * per_group]) for g in range(GROUPS)]

    def blocks_of(values):
        return [None if v is None else v[i * chunk : (i + 1) * chunk] for v in values for i in range(per_group)]

    def pick(values):
        return over_rows(select, jnp.concatenate(values, axis=0)).astype(BF16).reshape(n_dp, tok_count, part)

    def give_back(picked):
        got = {k: features.swap(picked[k], k) for k in distances}
        return [picked[0]] + [got[k] for k in range(1, n_dp)]

    def placed(pieces):
        result = jnp.zeros((tok_count, width), BF16)
        for k, piece in enumerate(pieces):
            result = lax.dynamic_update_slice(result, piece, (0, (here ^ k) * part))
        return result

    rows = grouped(exchange(dispatch(got_rows), bits)[0])
    sent_grads = dispatch(got_grads)
    grads = None
    sums, pre = [], [None] * GROUPS
    hidden, out, both, back = [None] * GROUPS, [None] * GROUPS, [None] * GROUPS, [None] * GROUPS

    def finish(item, *others):
        kind, gs = ITEMS[item]
        got = sums[item].result(*others)
        size = got.shape[0] // len(gs)
        for i, g in enumerate(gs):
            value = got[i * size : (i + 1) * size]
            if kind == "pre":
                pre[g] = value
                pre_gate, pre_up = value[:, :hidden_units], value[:, hidden_units:]
                hidden[g] = after((pre_gate * jax.nn.sigmoid(pre_gate) * pre_up).astype(BF16))
                out[g] = across(hidden[g], w_down).astype(BF16)
            else:
                pre_gate, pre_up = pre[g][:, :hidden_units], pre[g][:, hidden_units:]
                sig = jax.nn.sigmoid(pre_gate)
                pg_grad = (value * pre_up * sig * (1.0 + pre_gate * (1.0 - sig))).astype(BF16)
                pu_grad = (value * (pre_gate * sig)).astype(BF16)
                both[g] = after(jnp.concatenate([pg_grad, pu_grad], axis=1))
                back[g] = across(both[g], w_both).astype(BF16)

    def start(item):
        kind, gs = ITEMS[item]
        moved = joined([(rows if kind == "pre" else grads)[g] for g in gs])
        moved = after(moved, inward[item - AHEAD] if item >= AHEAD else got_grads[1])
        sums.append(LineSum("dp", jnp.dot(moved, w_both if kind == "pre" else w_down, preferred_element_type=F32)))
        inward.append(sums[item].inward())
        middle.append(sums[item].middle())

    inward, middle = [], []
    start(0)
    grads = grouped(exchange(sent_grads, bits, inward[0])[0])
    start(1)
    sums[0].outward()
    start(2)
    sums[1].outward()
    finish(0)
    start(3)
    sums[2].outward()
    finish(1)
    start(4)
    sums[3].outward()
    finish(2)
    halfway, half_o = exchange(blocks_of(out), bits[:1])
    start(5)
    sums[4].outward()
    finish(3, inward[4])
    here_blocks = blocks_of(out)
    out, arrived = exchange([block if half is None else half for block, half in zip(here_blocks, halfway)], bits[1:])
    sums[5].outward()
    finish(4, inward[5], half_o)
    halfway, arrived = exchange(blocks_of(back), bits[:1])
    out = give_back(pick(out))
    finish(5, out[1])
    here_blocks = blocks_of(back)
    back, _ = exchange([block if half is None else half for block, half in zip(here_blocks, halfway)], bits[1:], *out[1:])
    picked = pick(back)
    back = give_back(picked)

    mixed = placed([(piece.astype(F32) * gates).astype(BF16) for piece in out])
    token_grad = placed(back)
    all_rows, all_grads = jnp.concatenate(rows, axis=0), jnp.concatenate(grads, axis=0)
    all_both, all_hidden = jnp.concatenate(both, axis=0), jnp.concatenate(hidden, axis=0)
    all_both, all_hidden, _ = lax.optimization_barrier((all_both, all_hidden, picked))
    gate_grad = over_rows(all_rows, all_both[:, :hidden_units]).astype(BF16)
    up_grad = over_rows(all_rows, all_both[:, hidden_units:]).astype(BF16)
    down_grad = over_rows(all_grads, all_hidden).astype(BF16)
    return (mixed, token_grad, gate_grad[None], up_grad[None], down_grad[None])


def solution(mesh):
    rows = P(("groups", "expert", "dp"), None)
    weights = P("expert", "dp", None)
    grads = P(("groups", "expert"), "dp", None)
    return jax.shard_map(
        shards,
        mesh=mesh,
        in_specs=(rows, rows, rows, weights, weights, weights, rows),
        out_specs=(rows, rows, grads, grads, grads),
        check_vma=False,
    )
```

```python
import jax
import jax.numpy as jnp
from jax import lax
from jax.sharding import PartitionSpec as P

F32 = jnp.float32
BF16 = jnp.bfloat16
GROUPS = 4
CODE_ROWS = 16
ITEMS = (('pre', (0,)), ('pre', (2,)), ('pre', (3,)), ('pre', (1,)), ('hid', (2, 3)), ('hid', (0, 1)))


def route_codes(routes, capacity):
    ids = routes.reshape(-1)
    place = jnp.arange(ids.shape[0], dtype=jnp.int32)
    before = (ids[:, None] == ids[None, :]) & (place[:, None] < place[None, :])
    return ids * capacity + jnp.sum(before.astype(jnp.int32), axis=0)


def across(left, right):
    return lax.dot_general(left, right, (((1,), (1,)), ((), ())), preferred_element_type=F32)


def over_rows(left, right):
    return lax.dot_general(left, right, (((0,), (0,)), ((), ())), preferred_element_type=F32)


def joined(values, axis=0):
    return values[0] if len(values) == 1 else jnp.concatenate(values, axis=axis)


def after(value, *others):
    return lax.optimization_barrier((value, *others))[0]


class Queue:
    def __init__(self, axis, depth):
        self.axis, self.depth, self.arrived = axis, depth, []

    def turn(self, value):
        return after(value, *self.arrived[-self.depth :][:1]) if len(self.arrived) >= self.depth > 0 else value

    def send(self, value, pairs):
        got = lax.ppermute(self.turn(value), self.axis, pairs)
        self.arrived.append(got)
        return got

    def swap(self, value, distance):
        count = lax.axis_size(self.axis)
        return self.send(value, [(i, i ^ distance) for i in range(count)])


class LineSum:
    def __init__(self, axis, own):
        self.axis, self.count, self.own, self.total = axis, lax.axis_size(axis), own, own
        self.got = None

    def inward(self, *others):
        for hop in range(self.count // 2 - 1):
            pairs = [(hop, hop + 1), (self.count - 1 - hop, self.count - 2 - hop)]
            arrived = lax.ppermute(self.total.astype(BF16), self.axis, pairs)
            self.total = self.total + after(arrived, *others).astype(F32)
        return arrived

    def middle(self, *others):
        mid = self.count // 2
        self.total = after(self.total, *others)
        self.got = lax.ppermute(self.total.astype(BF16), self.axis, [(mid - 1, mid), (mid, mid - 1)])
        return self.got

    def outward(self, *others):
        got = after(self.got, *others)
        for hop in reversed(range(self.count // 2 - 1)):
            pairs = [(hop + 1, hop), (self.count - 2 - hop, self.count - 1 - hop)]
            arrived = lax.ppermute((self.own + got.astype(F32)).astype(BF16), self.axis, pairs)
            got = got + arrived
        self.got = got
        return arrived

    def result(self, *others):
        return self.total + after(self.got, *others).astype(F32)


def shards(tokens, routes, gates, gate_weight, up_weight, down_weight, cotangent):
    n_exp = lax.axis_size("expert") * gate_weight.shape[0]
    n_dp = lax.axis_size("dp")
    me = lax.axis_index("expert")
    here = lax.axis_index("dp")
    tok_count, topk = routes.shape
    width = tokens.shape[1]
    part = width // n_dp
    hidden_units = gate_weight.shape[2]
    capacity = 3 * tok_count * topk // (2 * n_exp)
    chunk = n_dp * capacity
    per_group = n_exp // GROUPS
    w_gate, w_up, w_down = gate_weight[0], up_weight[0], down_weight[0]
    w_both = jnp.concatenate([w_gate, w_up], axis=1)
    distances = list(range(n_dp - 1, 0, -1))

    features, experts = Queue("dp", 0), Queue("expert", 0)
    blocks = here ^ jnp.arange(n_dp, dtype=jnp.int32)

    def columns(value, distance):
        return lax.dynamic_slice(value, (0, (here ^ distance) * part), (tok_count, part))

    def by_features(value, tail):
        pieces = [columns(value, k) for k in range(n_dp)]
        if tail is not None:
            pieces = [jnp.concatenate([piece, tail], axis=0) for piece in pieces]
        earlier = list(features.arrived)
        got = {k: features.swap(after(pieces[k], *earlier), k) for k in distances}
        return [pieces[0]] + [got[k] for k in range(1, n_dp)]

    codes = route_codes(routes, capacity).astype(BF16)
    tail = jnp.zeros((CODE_ROWS, part), BF16) + jnp.pad(codes, (0, part - tok_count))[None, :]
    weighted = (gates * cotangent.astype(F32)).astype(BF16)
    got_rows = by_features(tokens, tail)
    got_grads = by_features(weighted, None)

    gathered = jnp.concatenate(got_rows, axis=0)
    codes = gathered.reshape(n_dp, tok_count + CODE_ROWS, part)[:, tok_count, :tok_count].astype(jnp.int32)
    places = ((codes // capacity) ^ me) * chunk + blocks[:, None] * capacity + codes % capacity

    def chooser(places):
        return (jnp.arange(n_exp * chunk, dtype=jnp.int32)[:, None] == places.reshape(-1)[None, :]).astype(BF16)

    select = chooser(places)
    select_whole = chooser(places[blocks])
    select_tailed = chooser(jnp.pad(places, ((0, 0), (0, CODE_ROWS)), constant_values=-1))

    def dispatch(chosen, gathered):
        rows = jnp.dot(chosen, gathered, preferred_element_type=F32).astype(BF16)
        return rows.reshape(n_exp, chunk, part)

    def exchange(blocks, bits, *others):
        blocks = list(blocks)
        for bit in bits:
            moved = [k for k in range(n_exp) if k & bit]
            sent = jnp.concatenate([blocks[k] for k in moved], axis=0)
            got = experts.swap(after(sent, *others), bit)
            for i, k in enumerate(moved):
                blocks[k] = got[i * chunk : (i + 1) * chunk]
            last = got
        return blocks, last

    bits = [n_exp >> (i + 1) for i in range(n_exp.bit_length() - 1)]

    def grouped(blocks):
        return [joined(blocks[g * per_group : (g + 1) * per_group]) for g in range(GROUPS)]

    def blocks_of(values):
        return [None if v is None else v[i * chunk : (i + 1) * chunk] for v in values for i in range(per_group)]

    def pick(values, select=select):
        return over_rows(select, jnp.concatenate(values, axis=0)).astype(BF16)

    def give_back_whole(picked):
        got = lax.all_to_all(picked.reshape(n_dp, tok_count, part), "dp", split_axis=0, concat_axis=0, tiled=False)
        return [got] * n_dp

    def give_back(picked):
        picked = picked.reshape(n_dp, tok_count, part)
        got = {k: features.swap(picked[k], k) for k in distances}
        return [picked[0]] + [got[k] for k in range(1, n_dp)]

    def placed(pieces):
        result = jnp.zeros((tok_count, width), BF16)
        for k, piece in enumerate(pieces):
            result = lax.dynamic_update_slice(result, piece, (0, (here ^ k) * part))
        return result

    rows = grouped(exchange(dispatch(select_tailed, gathered), bits)[0])
    sent_grads = dispatch(select, jnp.concatenate(got_grads, axis=0))
    grads = None
    sums, pre = [], [None] * GROUPS
    hidden, out, both, back = [None] * GROUPS, [None] * GROUPS, [None] * GROUPS, [None] * GROUPS

    def finish(item, *others):
        kind, gs = ITEMS[item]
        got = sums[item].result(*others)
        size = got.shape[0] // len(gs)
        for i, g in enumerate(gs):
            value = got[i * size : (i + 1) * size]
            if kind == "pre":
                pre[g] = value
                pre_gate, pre_up = value[:, :hidden_units], value[:, hidden_units:]
                hidden[g] = after((pre_gate * jax.nn.sigmoid(pre_gate) * pre_up).astype(BF16))
                out[g] = across(hidden[g], w_down).astype(BF16)
            else:
                pre_gate, pre_up = pre[g][:, :hidden_units], pre[g][:, hidden_units:]
                sig = jax.nn.sigmoid(pre_gate)
                pg_grad = (value * pre_up * sig * (1.0 + pre_gate * (1.0 - sig))).astype(BF16)
                pu_grad = (value * (pre_gate * sig)).astype(BF16)
                both[g] = after(jnp.concatenate([pg_grad, pu_grad], axis=1))
                back[g] = across(both[g], w_both).astype(BF16)

    def start(item):
        kind, gs = ITEMS[item]
        moved = joined([(rows if kind == "pre" else grads)[g] for g in gs])
        ahead = 2
        moved = after(moved, inward[item - ahead]) if item >= ahead else after(moved, got_grads[1])
        sums.append(LineSum("dp", jnp.dot(moved, w_both if kind == "pre" else w_down, preferred_element_type=F32)))
        inward.append(sums[item].inward(*inward[-1:]))
        middle.append(sums[item].middle())

    inward, middle, outward = [], [], []
    start(0)
    grads = grouped(exchange(sent_grads, bits, inward[0])[0])
    start(1)
    outward.append(sums[0].outward())
    start(2)
    outward.append(sums[1].outward(middle[0]))
    finish(0)
    start(3)
    outward.append(sums[2].outward(middle[1]))
    finish(1)
    start(4)
    outward.append(sums[3].outward(middle[2]))
    finish(2)
    halfway, half_o = exchange(blocks_of(out), bits[:1])
    start(5)
    outward.append(sums[4].outward(middle[3]))
    finish(3, inward[4])
    now = blocks_of(out)
    out, late_o = exchange([block if half is None else half for block, half in zip(now, halfway)], bits[1:])
    outward.append(sums[5].outward(middle[4]))
    picked = pick(out)
    sent_out = give_back(picked)
    finish(4, inward[5], half_o)
    halfway, half_g = exchange(blocks_of(back), bits[:1])
    finish(5, sent_out[1])
    now = blocks_of(back)
    moved, late_g = exchange([block if half is None else half for block, half in zip(now, halfway)], bits[1:])
    picked = pick(moved)
    all_both, all_hidden = jnp.concatenate(both, axis=0), jnp.concatenate(hidden, axis=0)
    all_both, all_hidden = lax.optimization_barrier((all_both, all_hidden))
    back = give_back(picked)
    out = sent_out

    all_both, all_hidden = after((all_both, all_hidden), back[1])
    mixed = placed([(piece.astype(F32) * gates).astype(BF16) for piece in out])
    token_grad = placed(back)
    all_rows, all_grads = jnp.concatenate(rows, axis=0), jnp.concatenate(grads, axis=0)
    gate_grad = over_rows(all_rows, all_both[:, :hidden_units]).astype(BF16)
    up_grad = over_rows(all_rows, all_both[:, hidden_units:]).astype(BF16)
    down_grad = over_rows(all_grads, all_hidden).astype(BF16)
    return (mixed, token_grad, gate_grad[None], up_grad[None], down_grad[None])


def solution(mesh):
    rows = P(("groups", "expert", "dp"), None)
    weights = P("expert", "dp", None)
    grads = P(("groups", "expert"), "dp", None)
    return jax.shard_map(
        shards,
        mesh=mesh,
        in_specs=(rows, rows, rows, weights, weights, weights, rows),
        out_specs=(rows, rows, grads, grads, grads),
        check_vma=False,
    )
```

```python
import jax
import jax.numpy as jnp
from jax import lax
from jax.sharding import PartitionSpec as P

F32 = jnp.float32
BF16 = jnp.bfloat16
GROUPS = 4
CODE_ROWS = 16
ITEMS = (('pre', (0,)), ('pre', (2,)), ('pre', (3,)), ('pre', (1,)), ('hid', (2, 3)), ('hid', (0, 1)))


def route_codes(routes, capacity):
    ids = routes.reshape(-1)
    place = jnp.arange(ids.shape[0], dtype=jnp.int32)
    before = (ids[:, None] == ids[None, :]) & (place[:, None] < place[None, :])
    return ids * capacity + jnp.sum(before.astype(jnp.int32), axis=0)


def across(left, right):
    return lax.dot_general(left, right, (((1,), (1,)), ((), ())), preferred_element_type=F32)


def over_rows(left, right):
    return lax.dot_general(left, right, (((0,), (0,)), ((), ())), preferred_element_type=F32)


def joined(values, axis=0):
    return values[0] if len(values) == 1 else jnp.concatenate(values, axis=axis)


def after(value, *others):
    return lax.optimization_barrier((value, *others))[0]


class Queue:
    def __init__(self, axis, depth):
        self.axis, self.depth, self.arrived = axis, depth, []

    def turn(self, value):
        return after(value, *self.arrived[-self.depth :][:1]) if len(self.arrived) >= self.depth > 0 else value

    def send(self, value, pairs):
        got = lax.ppermute(self.turn(value), self.axis, pairs)
        self.arrived.append(got)
        return got

    def swap(self, value, distance):
        count = lax.axis_size(self.axis)
        return self.send(value, [(i, i ^ distance) for i in range(count)])


class LineSum:
    def __init__(self, axis, own):
        self.axis, self.count, self.own, self.total = axis, lax.axis_size(axis), own, own
        self.got = None

    def inward(self, *others):
        for hop in range(self.count // 2 - 1):
            pairs = [(hop, hop + 1), (self.count - 1 - hop, self.count - 2 - hop)]
            arrived = lax.ppermute(self.total.astype(BF16), self.axis, pairs)
            self.total = self.total + after(arrived, *others).astype(F32)
        return arrived

    def middle(self, *others):
        mid = self.count // 2
        self.total = after(self.total, *others)
        self.got = lax.ppermute(self.total.astype(BF16), self.axis, [(mid - 1, mid), (mid, mid - 1)])
        return self.got

    def outward(self, *others):
        got = after(self.got, *others)
        for hop in reversed(range(self.count // 2 - 1)):
            pairs = [(hop + 1, hop), (self.count - 2 - hop, self.count - 1 - hop)]
            arrived = lax.ppermute((self.own + got.astype(F32)).astype(BF16), self.axis, pairs)
            got = got + arrived
        self.got = got
        return arrived

    def result(self, *others):
        return self.total + after(self.got, *others).astype(F32)


def shards(tokens, routes, gates, gate_weight, up_weight, down_weight, cotangent):
    n_exp = lax.axis_size("expert") * gate_weight.shape[0]
    n_dp = lax.axis_size("dp")
    me = lax.axis_index("expert")
    here = lax.axis_index("dp")
    tok_count, topk = routes.shape
    width = tokens.shape[1]
    part = width // n_dp
    hidden_units = gate_weight.shape[2]
    capacity = 3 * tok_count * topk // (2 * n_exp)
    chunk = n_dp * capacity
    per_group = n_exp // GROUPS
    w_gate, w_up, w_down = gate_weight[0], up_weight[0], down_weight[0]
    w_both = jnp.concatenate([w_gate, w_up], axis=1)
    distances = list(range(1, n_dp))

    features, experts = Queue("dp", 0), Queue("expert", 0)
    blocks = here ^ jnp.arange(n_dp, dtype=jnp.int32)

    def columns(value, distance):
        return lax.dynamic_slice(value, (0, (here ^ distance) * part), (tok_count, part))

    def by_features(value, tail):
        pieces = [columns(value, k) for k in range(n_dp)]
        if tail is not None:
            pieces = [jnp.concatenate([piece, tail], axis=0) for piece in pieces]
        earlier = list(features.arrived)
        got = {k: features.swap(after(pieces[k], *earlier), k) for k in distances}
        return [pieces[0]] + [got[k] for k in range(1, n_dp)]

    codes = route_codes(routes, capacity).astype(BF16)
    tail = jnp.zeros((CODE_ROWS, part), BF16) + jnp.pad(codes, (0, part - tok_count))[None, :]
    weighted = (gates * cotangent.astype(F32)).astype(BF16)
    got_rows = by_features(tokens, tail)
    got_grads = by_features(weighted, None)

    gathered = after(jnp.concatenate(got_rows, axis=0), got_grads[1])
    codes = gathered.reshape(n_dp, tok_count + CODE_ROWS, part)[:, tok_count, :tok_count].astype(jnp.int32)
    places = ((codes // capacity) ^ me) * chunk + blocks[:, None] * capacity + codes % capacity

    def chooser(places):
        return (jnp.arange(n_exp * chunk, dtype=jnp.int32)[:, None] == places.reshape(-1)[None, :]).astype(BF16)

    select = chooser(places)
    select_whole = chooser(places[blocks])
    select_tailed = chooser(jnp.pad(places, ((0, 0), (0, CODE_ROWS)), constant_values=-1))

    def dispatch(chosen, gathered):
        rows = jnp.dot(chosen, gathered, preferred_element_type=F32).astype(BF16)
        return rows.reshape(n_exp, chunk, part)

    def exchange(blocks, bits, *others):
        blocks = list(blocks)
        for bit in bits:
            moved = [k for k in range(n_exp) if k & bit]
            sent = jnp.concatenate([blocks[k] for k in moved], axis=0)
            got = experts.swap(after(sent, *others), bit)
            for i, k in enumerate(moved):
                blocks[k] = got[i * chunk : (i + 1) * chunk]
            last = got
        return blocks, last

    bits = [n_exp >> (i + 1) for i in range(n_exp.bit_length() - 1)]

    def grouped(blocks):
        return [joined(blocks[g * per_group : (g + 1) * per_group]) for g in range(GROUPS)]

    def blocks_of(values):
        return [None if v is None else v[i * chunk : (i + 1) * chunk] for v in values for i in range(per_group)]

    def pick(values, select=select):
        return over_rows(select, jnp.concatenate(values, axis=0)).astype(BF16)

    def give_back_whole(picked):
        got = lax.all_to_all(picked.reshape(n_dp, tok_count, part), "dp", split_axis=0, concat_axis=0, tiled=False)
        return [got] * n_dp

    def give_back(picked):
        picked = picked.reshape(n_dp, tok_count, part)
        got = {k: features.swap(picked[k], k) for k in distances}
        return [picked[0]] + [got[k] for k in range(1, n_dp)]

    def placed(pieces):
        result = jnp.zeros((tok_count, width), BF16)
        for k, piece in enumerate(pieces):
            result = lax.dynamic_update_slice(result, piece, (0, (here ^ k) * part))
        return result

    rows = grouped(exchange(dispatch(select_tailed, gathered), bits)[0])
    sent_grads = dispatch(select, jnp.concatenate(got_grads, axis=0))
    grads = None
    sums, pre = [], [None] * GROUPS
    hidden, out, both, back = [None] * GROUPS, [None] * GROUPS, [None] * GROUPS, [None] * GROUPS

    def finish(item, *others):
        kind, gs = ITEMS[item]
        got = sums[item].result(*others)
        size = got.shape[0] // len(gs)
        for i, g in enumerate(gs):
            value = got[i * size : (i + 1) * size]
            if kind == "pre":
                pre[g] = value
                pre_gate, pre_up = value[:, :hidden_units], value[:, hidden_units:]
                hidden[g] = after((pre_gate * jax.nn.sigmoid(pre_gate) * pre_up).astype(BF16))
                out[g] = across(hidden[g], w_down).astype(BF16)
            else:
                pre_gate, pre_up = pre[g][:, :hidden_units], pre[g][:, hidden_units:]
                sig = jax.nn.sigmoid(pre_gate)
                pg_grad = (value * pre_up * sig * (1.0 + pre_gate * (1.0 - sig))).astype(BF16)
                pu_grad = (value * (pre_gate * sig)).astype(BF16)
                both[g] = after(jnp.concatenate([pg_grad, pu_grad], axis=1))
                back[g] = across(both[g], w_both).astype(BF16)

    def start(item):
        kind, gs = ITEMS[item]
        moved = joined([(rows if kind == "pre" else grads)[g] for g in gs])
        ahead = 2
        moved = after(moved, inward[item - ahead]) if item >= ahead else moved
        sums.append(LineSum("dp", jnp.dot(moved, w_both if kind == "pre" else w_down, preferred_element_type=F32)))
        inward.append(sums[item].inward(*inward[-1:]))
        middle.append(sums[item].middle())

    inward, middle, outward = [], [], []
    start(0)
    grads = grouped(exchange(sent_grads, bits, inward[0])[0])
    start(1)
    outward.append(sums[0].outward())
    start(2)
    outward.append(sums[1].outward(middle[0]))
    finish(0)
    start(3)
    outward.append(sums[2].outward(middle[1]))
    finish(1)
    start(4)
    outward.append(sums[3].outward(middle[2]))
    finish(2)
    halfway, half_o = exchange(blocks_of(out), bits[:1])
    start(5)
    outward.append(sums[4].outward(middle[3]))
    finish(3, inward[4])
    now = blocks_of(out)
    out, late_o = exchange([block if half is None else half for block, half in zip(now, halfway)], bits[1:])
    outward.append(sums[5].outward(middle[4]))
    picked = pick(out)
    sent_out = give_back(picked)
    finish(4, inward[5], half_o)
    halfway, half_g = exchange(blocks_of(back), bits[:1])
    finish(5, sent_out[1])
    now = blocks_of(back)
    moved, late_g = exchange([block if half is None else half for block, half in zip(now, halfway)], bits[1:])
    picked = pick(moved)
    all_both, all_hidden = jnp.concatenate(both, axis=0), jnp.concatenate(hidden, axis=0)
    all_both, all_hidden = lax.optimization_barrier((all_both, all_hidden))
    back = give_back(picked)
    out = sent_out

    all_both, all_hidden = after((all_both, all_hidden), back[1])
    mixed = placed([(piece.astype(F32) * gates).astype(BF16) for piece in out])
    token_grad = placed(back)
    all_rows, all_grads = jnp.concatenate(rows, axis=0), jnp.concatenate(grads, axis=0)
    gate_grad = over_rows(all_rows, all_both[:, :hidden_units]).astype(BF16)
    up_grad = over_rows(all_rows, all_both[:, hidden_units:]).astype(BF16)
    down_grad = over_rows(all_grads, all_hidden).astype(BF16)
    return (mixed, token_grad, gate_grad[None], up_grad[None], down_grad[None])


def solution(mesh):
    rows = P(("groups", "expert", "dp"), None)
    weights = P("expert", "dp", None)
    grads = P(("groups", "expert"), "dp", None)
    return jax.shard_map(
        shards,
        mesh=mesh,
        in_specs=(rows, rows, rows, weights, weights, weights, rows),
        out_specs=(rows, rows, grads, grads, grads),
        check_vma=False,
    )
```

```python
import jax
import jax.numpy as jnp
from jax import lax
from jax.sharding import PartitionSpec as P

F32 = jnp.float32
BF16 = jnp.bfloat16
GROUPS = 4
CODE_ROWS = 16
ITEMS = (('pre', (0,)), ('pre', (2,)), ('pre', (3,)), ('pre', (1,)), ('hid', (2, 3)), ('hid', (0, 1)))


def route_codes(routes, capacity):
    ids = routes.reshape(-1)
    place = jnp.arange(ids.shape[0], dtype=jnp.int32)
    before = (ids[:, None] == ids[None, :]) & (place[:, None] < place[None, :])
    return ids * capacity + jnp.sum(before.astype(jnp.int32), axis=0)


def across(left, right):
    return lax.dot_general(left, right, (((1,), (1,)), ((), ())), preferred_element_type=F32)


def over_rows(left, right):
    return lax.dot_general(left, right, (((0,), (0,)), ((), ())), preferred_element_type=F32)


def joined(values, axis=0):
    return values[0] if len(values) == 1 else jnp.concatenate(values, axis=axis)


def after(value, *others):
    return lax.optimization_barrier((value, *others))[0]


class Queue:
    def __init__(self, axis, depth):
        self.axis, self.depth, self.arrived = axis, depth, []

    def turn(self, value):
        return after(value, *self.arrived[-self.depth :][:1]) if len(self.arrived) >= self.depth > 0 else value

    def send(self, value, pairs):
        got = lax.ppermute(self.turn(value), self.axis, pairs)
        self.arrived.append(got)
        return got

    def swap(self, value, distance):
        count = lax.axis_size(self.axis)
        return self.send(value, [(i, i ^ distance) for i in range(count)])


class LineSum:
    def __init__(self, axis, own):
        self.axis, self.count, self.own, self.total = axis, lax.axis_size(axis), own, own
        self.got = None

    def inward(self, *others):
        for hop in range(self.count // 2 - 1):
            pairs = [(hop, hop + 1), (self.count - 1 - hop, self.count - 2 - hop)]
            arrived = lax.ppermute(self.total.astype(BF16), self.axis, pairs)
            self.total = self.total + after(arrived, *others).astype(F32)
        return arrived

    def middle(self, *others):
        mid = self.count // 2
        self.total = after(self.total, *others)
        self.got = lax.ppermute(self.total.astype(BF16), self.axis, [(mid - 1, mid), (mid, mid - 1)])
        return self.got

    def outward(self, *others):
        got = after(self.got, *others)
        for hop in reversed(range(self.count // 2 - 1)):
            pairs = [(hop + 1, hop), (self.count - 2 - hop, self.count - 1 - hop)]
            arrived = lax.ppermute((self.own + got.astype(F32)).astype(BF16), self.axis, pairs)
            got = got + arrived
        self.got = got
        return arrived

    def result(self, *others):
        return self.total + after(self.got, *others).astype(F32)


def shards(tokens, routes, gates, gate_weight, up_weight, down_weight, cotangent):
    n_exp = lax.axis_size("expert") * gate_weight.shape[0]
    n_dp = lax.axis_size("dp")
    me = lax.axis_index("expert")
    here = lax.axis_index("dp")
    tok_count, topk = routes.shape
    width = tokens.shape[1]
    part = width // n_dp
    hidden_units = gate_weight.shape[2]
    capacity = 3 * tok_count * topk // (2 * n_exp)
    chunk = n_dp * capacity
    per_group = n_exp // GROUPS
    w_gate, w_up, w_down = gate_weight[0], up_weight[0], down_weight[0]
    w_both = jnp.concatenate([w_gate, w_up], axis=1)
    distances = list(range(1, n_dp))

    features, experts = Queue("dp", 0), Queue("expert", 0)
    blocks = here ^ jnp.arange(n_dp, dtype=jnp.int32)

    def columns(value, distance):
        return lax.dynamic_slice(value, (0, (here ^ distance) * part), (tok_count, part))

    def by_features(value, tail):
        pieces = [columns(value, k) for k in range(n_dp)]
        if tail is not None:
            pieces = [jnp.concatenate([piece, tail], axis=0) for piece in pieces]
        earlier = list(features.arrived)
        got = {k: features.swap(after(pieces[k], *earlier), k) for k in distances}
        return [pieces[0]] + [got[k] for k in range(1, n_dp)]

    codes = route_codes(routes, capacity).astype(BF16)
    tail = jnp.zeros((CODE_ROWS, part), BF16) + jnp.pad(codes, (0, part - tok_count))[None, :]
    weighted = (gates * cotangent.astype(F32)).astype(BF16)
    got_rows = by_features(tokens, tail)
    got_grads = by_features(weighted, None)

    *tailed, _ = lax.optimization_barrier((*got_rows, got_grads[1]))
    gathered = jnp.concatenate(tailed, axis=0)
    codes = gathered.reshape(n_dp, tok_count + CODE_ROWS, part)[:, tok_count, :tok_count].astype(jnp.int32)
    places = ((codes // capacity) ^ me) * chunk + blocks[:, None] * capacity + codes % capacity

    def chooser(places):
        return (jnp.arange(n_exp * chunk, dtype=jnp.int32)[:, None] == places.reshape(-1)[None, :]).astype(BF16)

    select = chooser(places)
    select_tailed = chooser(jnp.pad(places, ((0, 0), (0, CODE_ROWS)), constant_values=-1))

    def dispatch(chosen, gathered):
        rows = jnp.dot(chosen, gathered, preferred_element_type=F32).astype(BF16)
        return rows.reshape(n_exp, chunk, part)

    def exchange(blocks, bits, *others):
        blocks = list(blocks)
        for bit in bits:
            moved = [k for k in range(n_exp) if k & bit]
            sent = jnp.concatenate([blocks[k] for k in moved], axis=0)
            got = experts.swap(after(sent, *others), bit)
            for i, k in enumerate(moved):
                blocks[k] = got[i * chunk : (i + 1) * chunk]
            last = got
        return blocks, last

    bits = [n_exp >> (i + 1) for i in range(n_exp.bit_length() - 1)]

    def grouped(blocks):
        return [joined(blocks[g * per_group : (g + 1) * per_group]) for g in range(GROUPS)]

    def blocks_of(values):
        return [None if v is None else v[i * chunk : (i + 1) * chunk] for v in values for i in range(per_group)]

    def pick(values):
        return over_rows(select, jnp.concatenate(values, axis=0)).astype(BF16)

    def give_back(picked):
        picked = picked.reshape(n_dp, tok_count, part)
        got = {k: features.swap(picked[k], k) for k in distances}
        return [picked[0]] + [got[k] for k in range(1, n_dp)]

    def placed(pieces):
        result = jnp.zeros((tok_count, width), BF16)
        for k, piece in enumerate(pieces):
            result = lax.dynamic_update_slice(result, piece, (0, (here ^ k) * part))
        return result

    rows = grouped(exchange(dispatch(select_tailed, gathered), bits)[0])
    sent_grads = dispatch(select, jnp.concatenate(got_grads, axis=0))
    grads = None
    sums, pre = [], [None] * GROUPS
    hidden, out, both, back = [None] * GROUPS, [None] * GROUPS, [None] * GROUPS, [None] * GROUPS

    def finish(item, *others):
        kind, gs = ITEMS[item]
        got = sums[item].result(*others)
        size = got.shape[0] // len(gs)
        for i, g in enumerate(gs):
            value = got[i * size : (i + 1) * size]
            if kind == "pre":
                pre[g] = value
                pre_gate, pre_up = value[:, :hidden_units], value[:, hidden_units:]
                hidden[g] = after((pre_gate * jax.nn.sigmoid(pre_gate) * pre_up).astype(BF16))
                out[g] = across(hidden[g], w_down).astype(BF16)
            else:
                pre_gate, pre_up = pre[g][:, :hidden_units], pre[g][:, hidden_units:]
                sig = jax.nn.sigmoid(pre_gate)
                pg_grad = (value * pre_up * sig * (1.0 + pre_gate * (1.0 - sig))).astype(BF16)
                pu_grad = (value * (pre_gate * sig)).astype(BF16)
                both[g] = after(jnp.concatenate([pg_grad, pu_grad], axis=1))
                back[g] = across(both[g], w_both).astype(BF16)

    def start(item):
        kind, gs = ITEMS[item]
        moved = joined([(rows if kind == "pre" else grads)[g] for g in gs])
        ahead = 2
        moved = after(moved, inward[item - ahead]) if item >= ahead else moved
        sums.append(LineSum("dp", jnp.dot(moved, w_both if kind == "pre" else w_down, preferred_element_type=F32)))
        inward.append(sums[item].inward(*inward[-1:]))
        middle.append(sums[item].middle())

    inward, middle, outward = [], [], []
    start(0)
    grads = grouped(exchange(sent_grads, bits, inward[0])[0])
    start(1)
    outward.append(sums[0].outward())
    start(2)
    outward.append(sums[1].outward(middle[0]))
    finish(0)
    start(3)
    outward.append(sums[2].outward(middle[1]))
    finish(1)
    start(4)
    outward.append(sums[3].outward(middle[2]))
    finish(2)
    halfway, half_o = exchange(blocks_of(out), bits[:1])
    start(5)
    outward.append(sums[4].outward(middle[3]))
    finish(3, inward[4])
    now = blocks_of(out)
    out, late_o = exchange([block if half is None else half for block, half in zip(now, halfway)], bits[1:])
    outward.append(sums[5].outward(middle[4]))
    picked = pick(out)
    sent_out = give_back(picked)
    finish(4, inward[5], half_o)
    halfway, half_g = exchange(blocks_of(back), bits[:1])
    finish(5, sent_out[1])
    now = blocks_of(back)
    moved, late_g = exchange([block if half is None else half for block, half in zip(now, halfway)], bits[1:])
    picked = pick(moved)
    all_both, all_hidden = jnp.concatenate(both, axis=0), jnp.concatenate(hidden, axis=0)
    all_both, all_hidden = lax.optimization_barrier((all_both, all_hidden))
    back = give_back(picked)
    out = sent_out

    all_both, all_hidden = after((all_both, all_hidden), back[1])
    mixed = placed([(piece.astype(F32) * gates).astype(BF16) for piece in out])
    token_grad = placed(back)
    all_rows, all_grads = jnp.concatenate(rows, axis=0), jnp.concatenate(grads, axis=0)
    gate_grad = over_rows(all_rows, all_both[:, :hidden_units]).astype(BF16)
    up_grad = over_rows(all_rows, all_both[:, hidden_units:]).astype(BF16)
    down_grad = over_rows(all_grads, all_hidden).astype(BF16)
    return (mixed, token_grad, gate_grad[None], up_grad[None], down_grad[None])


def solution(mesh):
    rows = P(("groups", "expert", "dp"), None)
    weights = P("expert", "dp", None)
    grads = P(("groups", "expert"), "dp", None)
    return jax.shard_map(
        shards,
        mesh=mesh,
        in_specs=(rows, rows, rows, weights, weights, weights, rows),
        out_specs=(rows, rows, grads, grads, grads),
        check_vma=False,
    )
```

```python
import jax
import jax.numpy as jnp
from jax import lax
from jax.sharding import PartitionSpec as P

F32 = jnp.float32
BF16 = jnp.bfloat16
GROUPS = 4
CODE_ROWS = 16
ITEMS = (('pre', (0,)), ('pre', (2,)), ('pre', (3,)), ('pre', (1,)), ('hid', (2, 3)), ('hid', (0, 1)))


def route_codes(routes, capacity):
    ids = routes.reshape(-1)
    place = jnp.arange(ids.shape[0], dtype=jnp.int32)
    before = (ids[:, None] == ids[None, :]) & (place[:, None] < place[None, :])
    return ids * capacity + jnp.sum(before.astype(jnp.int32), axis=0)


def across(left, right):
    return lax.dot_general(left, right, (((1,), (1,)), ((), ())), preferred_element_type=F32)


def over_rows(left, right):
    return lax.dot_general(left, right, (((0,), (0,)), ((), ())), preferred_element_type=F32)


def joined(values, axis=0):
    return values[0] if len(values) == 1 else jnp.concatenate(values, axis=axis)


def after(value, *others):
    return lax.optimization_barrier((value, *others))[0]


class Queue:
    def __init__(self, axis, depth):
        self.axis, self.depth, self.arrived = axis, depth, []

    def turn(self, value):
        return after(value, *self.arrived[-self.depth :][:1]) if len(self.arrived) >= self.depth > 0 else value

    def send(self, value, pairs):
        got = lax.ppermute(self.turn(value), self.axis, pairs)
        self.arrived.append(got)
        return got

    def swap(self, value, distance):
        count = lax.axis_size(self.axis)
        return self.send(value, [(i, i ^ distance) for i in range(count)])


class LineSum:
    def __init__(self, axis, own):
        self.axis, self.count, self.own, self.total = axis, lax.axis_size(axis), own, own
        self.got = None

    def inward(self, *others):
        for hop in range(self.count // 2 - 1):
            pairs = [(hop, hop + 1), (self.count - 1 - hop, self.count - 2 - hop)]
            arrived = lax.ppermute(self.total.astype(BF16), self.axis, pairs)
            self.total = self.total + after(arrived, *others).astype(F32)
        return arrived

    def middle(self, *others):
        mid = self.count // 2
        self.total = after(self.total, *others)
        self.got = lax.ppermute(self.total.astype(BF16), self.axis, [(mid - 1, mid), (mid, mid - 1)])
        return self.got

    def outward(self, *others):
        got = after(self.got, *others)
        for hop in reversed(range(self.count // 2 - 1)):
            pairs = [(hop + 1, hop), (self.count - 2 - hop, self.count - 1 - hop)]
            arrived = lax.ppermute((self.own + got.astype(F32)).astype(BF16), self.axis, pairs)
            got = got + arrived
        self.got = got
        return arrived

    def result(self, *others):
        return self.total + after(self.got, *others).astype(F32)


def shards(tokens, routes, gates, gate_weight, up_weight, down_weight, cotangent):
    n_exp = lax.axis_size("expert") * gate_weight.shape[0]
    n_dp = lax.axis_size("dp")
    me = lax.axis_index("expert")
    here = lax.axis_index("dp")
    tok_count, topk = routes.shape
    width = tokens.shape[1]
    part = width // n_dp
    hidden_units = gate_weight.shape[2]
    capacity = 3 * tok_count * topk // (2 * n_exp)
    chunk = n_dp * capacity
    per_group = n_exp // GROUPS
    w_gate, w_up, w_down = gate_weight[0], up_weight[0], down_weight[0]
    w_both = jnp.concatenate([w_gate, w_up], axis=1)
    distances = list(range(1, n_dp))

    features, experts = Queue("dp", 0), Queue("expert", 0)
    blocks = here ^ jnp.arange(n_dp, dtype=jnp.int32)

    def columns(value, distance):
        return lax.dynamic_slice(value, (0, (here ^ distance) * part), (tok_count, part))

    def by_features(value, tail):
        pieces = [columns(value, k) for k in range(n_dp)]
        if tail is not None:
            pieces = [jnp.concatenate([piece, tail], axis=0) for piece in pieces]
        earlier = list(features.arrived)
        got = {k: features.swap(after(pieces[k], *earlier), k) for k in distances}
        return [pieces[0]] + [got[k] for k in range(1, n_dp)]

    codes = route_codes(routes, capacity).astype(BF16)
    tail = jnp.zeros((CODE_ROWS, part), BF16) + jnp.pad(codes, (0, part - tok_count))[None, :]
    weighted = (gates * cotangent.astype(F32)).astype(BF16)
    got_rows = by_features(tokens, tail)
    got_grads = by_features(weighted, None)

    *tailed, _ = lax.optimization_barrier((*got_rows, got_grads[1]))
    gathered = jnp.concatenate(tailed, axis=0)
    codes = gathered.reshape(n_dp, tok_count + CODE_ROWS, part)[:, tok_count, :tok_count].astype(jnp.int32)
    places = ((codes // capacity) ^ me) * chunk + blocks[:, None] * capacity + codes % capacity

    def chooser(places):
        return (jnp.arange(n_exp * chunk, dtype=jnp.int32)[:, None] == places.reshape(-1)[None, :]).astype(BF16)

    select = chooser(places)
    select_tailed = chooser(jnp.pad(places, ((0, 0), (0, CODE_ROWS)), constant_values=-1))

    def dispatch(chosen, gathered):
        rows = jnp.dot(chosen, gathered, preferred_element_type=F32).astype(BF16)
        return rows.reshape(n_exp, chunk, part)

    def exchange(blocks, bits, *others):
        blocks = list(blocks)
        for bit in bits:
            moved = [k for k in range(n_exp) if k & bit]
            sent = jnp.concatenate([blocks[k] for k in moved], axis=0)
            got = experts.swap(after(sent, *others), bit)
            for i, k in enumerate(moved):
                blocks[k] = got[i * chunk : (i + 1) * chunk]
            last = got
        return blocks, last

    bits = [n_exp >> (i + 1) for i in range(n_exp.bit_length() - 1)]

    def grouped(blocks):
        return [joined(blocks[g * per_group : (g + 1) * per_group]) for g in range(GROUPS)]

    def blocks_of(values):
        return [None if v is None else v[i * chunk : (i + 1) * chunk] for v in values for i in range(per_group)]

    def pick(values):
        return over_rows(select, jnp.concatenate(values, axis=0)).astype(BF16)

    def give_back(picked):
        picked = picked.reshape(n_dp, tok_count, part)
        got = {k: features.swap(picked[k], k) for k in distances}
        return [picked[0]] + [got[k] for k in range(1, n_dp)]

    def placed(pieces):
        result = jnp.zeros((tok_count, width), BF16)
        for k, piece in enumerate(pieces):
            result = lax.dynamic_update_slice(result, piece, (0, (here ^ k) * part))
        return result

    sent_rows = dispatch(select_tailed, gathered)
    ahead = (jnp.dot(sent_rows[0], w_both, preferred_element_type=F32),) if per_group == 1 else ()
    rows = grouped(exchange(sent_rows, bits, *ahead)[0])
    sent_grads = dispatch(select, jnp.concatenate(got_grads, axis=0))
    grads = None
    sums, pre = [], [None] * GROUPS
    hidden, out, both, back = [None] * GROUPS, [None] * GROUPS, [None] * GROUPS, [None] * GROUPS

    def finish(item, *others):
        kind, gs = ITEMS[item]
        got = sums[item].result(*others)
        size = got.shape[0] // len(gs)
        for i, g in enumerate(gs):
            value = got[i * size : (i + 1) * size]
            if kind == "pre":
                pre[g] = value
                pre_gate, pre_up = value[:, :hidden_units], value[:, hidden_units:]
                hidden[g] = after((pre_gate * jax.nn.sigmoid(pre_gate) * pre_up).astype(BF16))
                out[g] = across(hidden[g], w_down).astype(BF16)
            else:
                pre_gate, pre_up = pre[g][:, :hidden_units], pre[g][:, hidden_units:]
                sig = jax.nn.sigmoid(pre_gate)
                pg_grad = (value * pre_up * sig * (1.0 + pre_gate * (1.0 - sig))).astype(BF16)
                pu_grad = (value * (pre_gate * sig)).astype(BF16)
                both[g] = after(jnp.concatenate([pg_grad, pu_grad], axis=1))
                back[g] = across(both[g], w_both).astype(BF16)

    def start(item):
        kind, gs = ITEMS[item]
        moved = joined([(rows if kind == "pre" else grads)[g] for g in gs])
        ahead = 2
        moved = after(moved, inward[item - ahead]) if item >= ahead else moved
        sums.append(LineSum("dp", jnp.dot(moved, w_both if kind == "pre" else w_down, preferred_element_type=F32)))
        inward.append(sums[item].inward(*inward[-1:]))
        middle.append(sums[item].middle())

    inward, middle, outward = [], [], []
    start(0)
    grads = grouped(exchange(sent_grads, bits, inward[0])[0])
    start(1)
    outward.append(sums[0].outward())
    start(2)
    outward.append(sums[1].outward(middle[0]))
    finish(0)
    start(3)
    outward.append(sums[2].outward(middle[1]))
    finish(1)
    start(4)
    outward.append(sums[3].outward(middle[2]))
    finish(2)
    halfway, half_o = exchange(blocks_of(out), bits[:1])
    start(5)
    outward.append(sums[4].outward(middle[3]))
    finish(3, inward[4])
    now = blocks_of(out)
    out, late_o = exchange([block if half is None else half for block, half in zip(now, halfway)], bits[1:])
    outward.append(sums[5].outward(middle[4]))
    picked = pick(out)
    sent_out = give_back(picked)
    finish(4, inward[5], half_o)
    halfway, half_g = exchange(blocks_of(back), bits[:1])
    finish(5, sent_out[1])
    now = blocks_of(back)
    moved, late_g = exchange([block if half is None else half for block, half in zip(now, halfway)], bits[1:])
    picked = pick(moved)
    all_both, all_hidden = jnp.concatenate(both, axis=0), jnp.concatenate(hidden, axis=0)
    all_both, all_hidden = lax.optimization_barrier((all_both, all_hidden))
    back = give_back(picked)
    out = sent_out

    all_both, all_hidden = after((all_both, all_hidden), back[1])
    mixed = placed([(piece.astype(F32) * gates).astype(BF16) for piece in out])
    token_grad = placed(back)
    all_rows, all_grads = jnp.concatenate(rows, axis=0), jnp.concatenate(grads, axis=0)
    gate_grad = over_rows(all_rows, all_both[:, :hidden_units]).astype(BF16)
    up_grad = over_rows(all_rows, all_both[:, hidden_units:]).astype(BF16)
    down_grad = over_rows(all_grads, all_hidden).astype(BF16)
    return (mixed, token_grad, gate_grad[None], up_grad[None], down_grad[None])


def solution(mesh):
    rows = P(("groups", "expert", "dp"), None)
    weights = P("expert", "dp", None)
    grads = P(("groups", "expert"), "dp", None)
    return jax.shard_map(
        shards,
        mesh=mesh,
        in_specs=(rows, rows, rows, weights, weights, weights, rows),
        out_specs=(rows, rows, grads, grads, grads),
        check_vma=False,
    )
```
